512 devices in a mesh: seq: 32 (over y, x, core), head: 16 (over z).
Axes of the slice: x: 4, y: 4, z: 16, core: 2. Of those that a mesh axis runs over, the one named last changes fastest.
Arguments:
- shared_qk: bfloat16 [65536, 2048], P('seq', 'head'), may hold values from -6 to 6
- values: bfloat16 [65536, 2048], P('seq', 'head'), may hold values from -6 to 6
- cotangent: bfloat16 [65536, 2048], P('seq', 'head'), may hold values from -6 to 6
- cluster_ids: int32 [512], replicated, may hold values from 0 to 511, as said below
- neighbour: int32 [512], replicated, may hold values from -1 to 511, as said below
Outputs:
- grad_qk: bfloat16 [65536, 2048], P('seq', 'head')
- grad_values: bfloat16 [65536, 2048], P('seq', 'head')
The draws below stay inside these ranges and needn't reach their ends.
Inputs may be any that keep to these rules, and one draw needn't show every extreme that they name: `cluster_ids`: clusters g * 16 to (g + 1) * 16 - 1 form group g. The 16 blocks of one seq index go to 16 groups, exactly 1 to each; every group receives exactly 16 blocks. A cluster holds at most 2 blocks, and in each group as many clusters hold 2 blocks as hold none. `neighbour`: each entry is -1 or the cluster 1 ids further along in the same group, cyclically.
All inputs are finite; a program needn't handle non-finite values.
Results may differ from the reference program's by a relative error of at most 0.0094.
Values may be sent and summed in bfloat16 or wider, within the bound.
No kernel may reach another device: no remote copies, remote signals or barrier semaphores. Data moves between devices by JAX's collectives and lax.ppermute only.
A program may use at most 64 MiB of HBM per device.

```python
import math
import jax
import jax.numpy as jnp
from jax import lax

BLOCK = 128
DH = 128
HEADS = 16
CAPC = 2
BPD = 16
TOKENS = 65536
SLOT = 1
CPD = 1
NCL = 512


def draw_shared_qk(key, part):
    key = jax.random.fold_in(key, 11)
    key_base = jax.random.fold_in(key, 0)
    return jax.random.truncated_normal(key_base, -6.0, 6.0, (TOKENS, HEADS * DH), jnp.float32).astype(jnp.bfloat16)


def draw_cluster_ids(key, part):
    key = jax.random.fold_in(key, 5)
    key_offsets, key_order, key_full, key_sizes, key_mix = jax.random.split(key, 5)
    groups = NCL // BPD
    used = BPD // SLOT
    ranks = jax.random.permutation(key_offsets, groups).astype(jnp.int32)
    choices_all = jnp.arange(groups, dtype=jnp.int32)
    ranks = jnp.where(choices_all == 1, -3, ranks)
    ranks = jnp.where(choices_all == groups - 1, -2, ranks)
    ranks = jnp.where(choices_all == groups // 2, -1, ranks)
    offsets = jnp.argsort(ranks)[:used].astype(jnp.int32)
    orders = jax.vmap(lambda subkey: jax.random.permutation(subkey, BPD))(jax.random.split(key_order, groups))
    column = jnp.arange(BPD) // SLOT
    destined = (jnp.arange(groups)[:, None] + offsets[column][None, :]) % groups
    row_ids = jnp.broadcast_to(jnp.arange(groups)[:, None], (groups, BPD))
    group = jnp.zeros((groups, BPD), jnp.int32).at[row_ids, orders].set(destined.astype(jnp.int32)).reshape(-1)
    count = groups * BPD
    indices = jnp.arange(count)
    earlier = indices[None, :] < indices[:, None]
    arrival = jnp.sum((earlier & (group[:, None] == group[None, :])).astype(jnp.int32), axis=1)
    full = jax.random.randint(key_full, (groups, 1), 1, BPD // 4 + 1)
    slots = jnp.arange(BPD)[None, :]
    base = jnp.where(slots < full, 2, jnp.where(slots < 2 * full, 0, 1)).astype(jnp.int32)
    cluster_sizes = jax.vmap(jax.random.permutation)(jax.random.split(key_sizes, groups), base)
    bounds = jnp.cumsum(cluster_sizes, axis=1)
    members = jnp.sum((bounds[:, None, :] <= jnp.arange(BPD)[None, :, None]).astype(jnp.int32), axis=2)
    mixed = jax.vmap(jax.random.permutation)(jax.random.split(key_mix, groups), members)
    local = mixed[group, arrival]
    return (group * BPD + local).astype(jnp.int32)


def draw_neighbour(key, part):
    key = jax.random.fold_in(key, 7)
    indices = jnp.arange(NCL, dtype=jnp.int32)
    group_base = indices // BPD * BPD
    following = group_base + (indices - group_base + CPD) % BPD
    keep = jax.random.randint(key, (NCL,), 0, 4) > 0
    return jnp.where(keep, following, -1).astype(jnp.int32)


def steps_of(stream_key, shape, pieces, smallest, top_value):
    def one(axis_at, blocks):
        steps = jax.random.uniform(jax.random.fold_in(jax.random.fold_in(stream_key, 6), axis_at), (blocks,), jnp.float32, smallest / len(pieces), top_value / len(pieces))
        return jnp.repeat(jnp.exp(steps), shape[axis_at] // blocks).reshape((-1,) + (1,) * (len(shape) - axis_at - 1))

    level = one(*pieces[0])
    for cut in pieces[1:]:
        level = level * one(*cut)
    return level


def bell_draw(stream_key, extent, spread, bound, shards=(), kind=jnp.bfloat16):
    drawn = spread * jax.random.normal(stream_key, extent, jnp.float32)
    if shards:
        drawn = drawn * steps_of(stream_key, extent, shards, -0.22, 0.18)
    return jnp.clip(drawn, -bound, bound).astype(kind)


def setup_inputs(seed: int = 0) -> dict:
    key_of = jax.random.split(jax.random.key(seed), 6)
    return {
        "shared_qk": draw_shared_qk(jax.random.fold_in(key_of[5], 71), 0),
        "values": bell_draw(key_of[1], (TOKENS, HEADS * DH), 1.0, 6.0, ((0, 32), (1, 16))),
        "cotangent": bell_draw(key_of[2], (TOKENS, HEADS * DH), 1.0, 6.0, ((0, 32), (1, 16))),
        "cluster_ids": draw_cluster_ids(jax.random.fold_in(key_of[5], 71), 0),
        "neighbour": draw_neighbour(jax.random.fold_in(key_of[5], 71), 0),
    }


def attend(query_local_rows, value_own, cotangent_local_rows, query_near, value_near, own_ok, near_ok):
    row_count = query_local_rows.shape[1]
    score_scale_factor = 1.0 / math.sqrt(query_local_rows.shape[2])
    key_matrix_rows = jnp.concatenate([query_local_rows, query_near], axis=1).astype(jnp.float32)
    value_matrix_rows = jnp.concatenate([value_own, value_near], axis=1).astype(jnp.float32)
    query_broad_rows = query_local_rows.astype(jnp.float32)
    cotangent_broad_rows = cotangent_local_rows.astype(jnp.float32)
    logit_scores = jnp.einsum('ylz,yez->yle', query_broad_rows, key_matrix_rows) * score_scale_factor
    key_ok = jnp.concatenate([own_ok, near_ok], axis=1)
    not_self = jnp.arange(2 * row_count)[None, :] != jnp.arange(row_count)[:, None]
    allowed = key_ok[:, None, :] & not_self[None, :, :]
    logit_scores = jnp.where(allowed, logit_scores, -1e+30)
    row_max = lax.optimization_barrier(jnp.max(logit_scores, axis=2, keepdims=True))
    weight = jnp.where(allowed, jnp.exp(logit_scores - row_max), 0.0)
    denominator = lax.optimization_barrier(jnp.sum(weight, axis=2, keepdims=True)) + jnp.where(own_ok, 0.0, 1.0)[:, :, None]
    probs = weight / denominator
    probabilities_reduced = lax.optimization_barrier(probs.astype(jnp.bfloat16)).astype(jnp.float32)
    attended_output = jnp.einsum('ynp,ypm->ynm', probabilities_reduced, value_matrix_rows)
    delta = lax.optimization_barrier(jnp.sum(cotangent_broad_rows * attended_output, axis=2, keepdims=True))
    probability_gradient = jnp.einsum('ylz,yez->yle', cotangent_broad_rows, value_matrix_rows)
    score_gradient = lax.optimization_barrier((probs * (probability_gradient - delta) * score_scale_factor).astype(jnp.bfloat16)).astype(jnp.float32)
    query_gradient = jnp.einsum('ynp,ypm->ynm', score_gradient, key_matrix_rows)
    key_gradient = jnp.einsum('eap,eas->eps', score_gradient, query_broad_rows)
    value_gradient = jnp.einsum('eap,eas->eps', probabilities_reduced, cotangent_broad_rows)
    own_qk = (query_gradient + key_gradient[:, :row_count]).astype(jnp.bfloat16)
    own_v = value_gradient[:, :row_count].astype(jnp.bfloat16)
    return (own_qk, own_v, key_gradient[:, row_count:].astype(jnp.bfloat16), value_gradient[:, row_count:].astype(jnp.bfloat16))

def reference(shared_qk, values, cotangent, cluster_ids, neighbour):
    block_count = TOKENS // BLOCK
    cluster_count = neighbour.shape[0]
    slot_rows = CAPC * BLOCK
    indices = jnp.arange(block_count, dtype=jnp.int32)
    earlier = indices[None, :] < indices[:, None]
    same_cluster = cluster_ids[:, None] == cluster_ids[None, :]
    position = lax.optimization_barrier(jnp.sum((earlier & same_cluster).astype(jnp.int32), axis=1))
    slot_key = (cluster_ids * CAPC + position).astype(jnp.int32)
    member = jnp.full((cluster_count * CAPC,), block_count, jnp.int32).at[slot_key].set(indices)
    cluster_sizes = jnp.zeros((cluster_count,), jnp.int32).at[cluster_ids].add(1)
    slot_ok = (jnp.arange(slot_rows) // BLOCK)[None, :] < cluster_sizes[:, None]
    has_near = neighbour >= 0
    near_index = jnp.where(has_near, neighbour, 0).astype(jnp.int32)
    near_ok = slot_ok[near_index] & has_near[:, None]
    target = jnp.where(has_near, neighbour, cluster_count).astype(jnp.int32)

    def to_tiles(field):
        blocks = field.reshape(block_count, BLOCK, DH)
        blocks = jnp.concatenate([blocks, jnp.zeros((1, BLOCK, DH), field.dtype)], axis=0)
        return blocks[member].reshape(cluster_count, slot_rows, DH)

    def settle(own, part):
        moved = jnp.zeros((cluster_count + 1, slot_rows, DH), jnp.float32).at[target].add(lax.optimization_barrier(part).astype(jnp.float32))
        total = (lax.optimization_barrier(own).astype(jnp.float32) + moved[:cluster_count]).astype(jnp.bfloat16)
        return total.reshape(cluster_count * CAPC, BLOCK, DH)[slot_key].reshape(TOKENS, DH)

    def per_head(fields):
        qk_head, value_head, cot_head = fields
        query_tiles = to_tiles(qk_head)
        value_tiles = to_tiles(value_head)
        cot_tiles = to_tiles(cot_head)
        own_qk, own_v, part_qk, part_v = attend(query_tiles, value_tiles, cot_tiles, query_tiles[near_index], value_tiles[near_index], slot_ok, near_ok)
        return (settle(own_qk, part_qk), settle(own_v, part_v))

    def heads_first(field):
        return field.reshape(TOKENS, HEADS, DH).transpose(1, 0, 2)
    grads_qk, grads_v = lax.map(per_head, (heads_first(shared_qk), heads_first(values), heads_first(cotangent)))
    grad_qk = grads_qk.transpose(1, 0, 2).reshape(TOKENS, HEADS * DH)
    grad_values = grads_v.transpose(1, 0, 2).reshape(TOKENS, HEADS * DH)
    return (grad_qk, grad_values)
```

```python
import functools
import math

import jax
import jax.numpy as jnp
from jax import lax
from jax.experimental import pallas as pl
from jax.experimental.pallas import tpu as pltpu
from jax.sharding import PartitionSpec as P

BLOCK = 128
DH = 128
NT = (((1,), (1,)), ((), ()))
NN = (((1,), (0,)), ((), ()))
TN = (((0,), (0,)), ((), ()))


def dot(a, b, dims):
    return lax.dot_general(a, b, dims, preferred_element_type=jnp.float32)


def pack_kernel(per_source, group_size, ids_ref, a_ref, b_ref, c_ref, out_ref, sems):
    base = lax.axis_index("seq") * per_source
    copies = []
    for i in range(per_source):
        slot = ids_ref[base + i] // group_size
        for j, ref in enumerate((a_ref, b_ref, c_ref)):
            copy = pltpu.make_async_copy(
                ref.at[pl.ds(i * BLOCK, BLOCK)], out_ref.at[slot, j], sems.at[i, j]
            )
            copy.start()
            copies.append(copy)
    for copy in copies:
        copy.wait()


def unpack_kernel(per_source, group_size, ids_ref, in_ref, a_ref, b_ref, sems):
    base = lax.axis_index("seq") * per_source
    copies = []
    for i in range(per_source):
        slot = ids_ref[base + i] // group_size
        for j, ref in enumerate((a_ref, b_ref)):
            copy = pltpu.make_async_copy(
                in_ref.at[slot, j], ref.at[pl.ds(i * BLOCK, BLOCK)], sems.at[i, j]
            )
            copy.start()
            copies.append(copy)
    for copy in copies:
        copy.wait()


def attend_kernel(clusters, table_ref, in_ref, out_ref, carry_ref, first_ref):
    scale = 1.0 / math.sqrt(DH)
    factor = scale * math.log2(math.e)

    def attend(c, following, have_part, own_count, near_count):
        own_src = [table_ref[1 + p, c] for p in range(own_count)]
        near_src = [table_ref[1 + p, following] for p in range(near_count)]
        sources = own_src + near_src
        keys = [in_ref[s, 0] for s in sources]
        vals = [in_ref[s, 1] for s in sources]
        q = jnp.concatenate(keys[:own_count], axis=0)
        g = jnp.concatenate([in_ref[s, 2] for s in own_src], axis=0)
        width = own_count * BLOCK
        ahead = lax.broadcasted_iota(jnp.int32, (BLOCK, width), 1) - lax.broadcasted_iota(
            jnp.int32, (BLOCK, width), 0
        )
        scores = [dot(k, q, NT) for k in keys]
        for p in range(own_count):
            scores[p] = jnp.where(ahead == p * BLOCK, -1e30, scores[p])
        top = functools.reduce(jnp.maximum, [jnp.max(s, axis=0, keepdims=True) for s in scores])
        weights = [jnp.exp2((s - top) * factor) for s in scores]
        dprobs = [dot(v, g, NT) for v in vals]
        total = sum(jnp.sum(w, axis=0, keepdims=True) for w in weights)
        inverse = 1.0 / total
        delta = (
            sum(jnp.sum(w * d, axis=0, keepdims=True) for w, d in zip(weights, dprobs)) * inverse
        )
        probs = [w * inverse for w in weights]
        dscores = [(p * (d - delta)).astype(jnp.bfloat16) for p, d in zip(probs, dprobs)]
        grad_w = [dot(p.astype(jnp.bfloat16), g, NN) for p in probs]
        grad_k = [dot(s, q, NN) for s in dscores]
        grad_q = dot(
            jnp.concatenate(dscores, axis=0), jnp.concatenate(keys, axis=0), TN
        )
        for p in range(own_count):
            own_qk = (grad_q[p * BLOCK : (p + 1) * BLOCK] + grad_k[p]) * scale
            own_v = grad_w[p]
            own_qk = own_qk + jnp.where(have_part, carry_ref[0, p], 0.0)
            own_v = own_v + jnp.where(have_part, carry_ref[1, p], 0.0)
            out_ref[own_src[p], 0] = own_qk.astype(jnp.bfloat16)
            out_ref[own_src[p], 1] = own_v.astype(jnp.bfloat16)

            @pl.when(c == 0)
            def _():
                first_ref[0, p] = own_qk
                first_ref[1, p] = own_v

        for p in range(near_count):
            carry_ref[0, p] = grad_k[own_count + p] * scale
            carry_ref[1, p] = grad_w[own_count + p]

    def step(c, have_part):
        following = lax.rem(c + 1, clusters)
        own = table_ref[0, c]
        near = jnp.where(table_ref[3, c] > 0, table_ref[0, following], 0)
        for own_count in (1, 2):
            for near_count in (0, 1, 2):

                @pl.when((own == own_count) & (near == near_count))
                def _():
                    attend(c, following, have_part > 0, own_count, near_count)

        return ((own > 0) & (near > 0)).astype(jnp.int32)

    have_part = lax.fori_loop(0, clusters, step, jnp.int32(0))
    for p in range(2):

        @pl.when((have_part > 0) & (table_ref[0, 0] > p))
        def _():
            source = table_ref[1 + p, 0]
            for j in range(2):
                out_ref[source, j] = (first_ref[j, p] + carry_ref[j, p]).astype(jnp.bfloat16)


def per_device(shared_qk, values, cotangent, cluster_ids, neighbour):
    n_seq = lax.axis_size("seq")
    seq_index = lax.axis_index("seq")
    tokens, lanes = shared_qk.shape
    per_source = tokens // BLOCK
    group_size = neighbour.shape[0] // n_seq
    any_space = pl.BlockSpec(memory_space=pl.ANY)
    smem = pl.BlockSpec(memory_space=pltpu.SMEM)
    vmem = pl.BlockSpec(memory_space=pltpu.VMEM)

    sent = pl.pallas_call(
        functools.partial(pack_kernel, per_source, group_size),
        out_shape=jax.ShapeDtypeStruct((n_seq, 3, BLOCK, lanes), shared_qk.dtype),
        in_specs=[smem, any_space, any_space, any_space],
        out_specs=any_space,
        scratch_shapes=[pltpu.SemaphoreType.DMA((per_source, 3))],
        name="pack",
    )(cluster_ids, shared_qk, values, cotangent)
    arrived = lax.all_to_all(sent, "seq", split_axis=0, concat_axis=0, tiled=True)

    local = seq_index * group_size + jnp.arange(group_size, dtype=jnp.int32)
    member = cluster_ids[None, :] == local[:, None]
    source = jnp.arange(cluster_ids.shape[0], dtype=jnp.int32)[None, :] // per_source
    table = jnp.stack(
        [
            jnp.sum(member.astype(jnp.int32), axis=1),
            jnp.min(jnp.where(member, source, n_seq - 1), axis=1),
            jnp.max(jnp.where(member, source, 0), axis=1),
            lax.dynamic_slice_in_dim(neighbour, seq_index * group_size, group_size) + 1,
        ]
    )
    returned = pl.pallas_call(
        functools.partial(attend_kernel, group_size),
        out_shape=jax.ShapeDtypeStruct((n_seq, 2, BLOCK, lanes), shared_qk.dtype),
        in_specs=[smem, vmem],
        out_specs=vmem,
        scratch_shapes=[
            pltpu.VMEM((2, 2, BLOCK, lanes), jnp.float32),
            pltpu.VMEM((2, 2, BLOCK, lanes), jnp.float32),
        ],
        compiler_params=pltpu.CompilerParams(vmem_limit_bytes=32 * 1024 * 1024),
        name="attend",
    )(table, arrived)
    home = lax.all_to_all(returned, "seq", split_axis=0, concat_axis=0, tiled=True)

    out = jax.ShapeDtypeStruct((tokens, lanes), shared_qk.dtype)
    return pl.pallas_call(
        functools.partial(unpack_kernel, per_source, group_size),
        out_shape=(out, out),
        in_specs=[smem, any_space],
        out_specs=(any_space, any_space),
        scratch_shapes=[pltpu.SemaphoreType.DMA((per_source, 2))],
        name="unpack",
    )(cluster_ids, home)


def solution(mesh):
    in_specs = (P("seq", "head"), P("seq", "head"), P("seq", "head"), P(), P())
    out_specs = (P("seq", "head"), P("seq", "head"))
    return jax.shard_map(
        per_device, mesh=mesh, in_specs=in_specs, out_specs=out_specs, check_vma=False
    )
```

```python
import functools
import math

import jax
import jax.numpy as jnp
from jax import lax
from jax.experimental import pallas as pl
from jax.experimental.pallas import tpu as pltpu
from jax.sharding import PartitionSpec as P

BLOCK = 128
DH = 128
NT = (((1,), (1,)), ((), ()))
NN = (((1,), (0,)), ((), ()))
TN = (((0,), (0,)), ((), ()))


def dot(a, b, dims):
    return lax.dot_general(a, b, dims, preferred_element_type=jnp.float32)


def pack_kernel(per_source, group_size, ids_ref, a_ref, b_ref, c_ref, out_ref, sems):
    base = lax.axis_index("seq") * per_source
    copies = []
    for i in range(per_source):
        slot = ids_ref[base + i] // group_size
        for j, ref in enumerate((a_ref, b_ref, c_ref)):
            copy = pltpu.make_async_copy(
                ref.at[pl.ds(i * BLOCK, BLOCK)], out_ref.at[slot, j], sems.at[i, j]
            )
            copy.start()
            copies.append(copy)
    for copy in copies:
        copy.wait()


def unpack_kernel(per_source, group_size, ids_ref, in_ref, a_ref, b_ref, sems):
    base = lax.axis_index("seq") * per_source
    copies = []
    for i in range(per_source):
        slot = ids_ref[base + i] // group_size
        for j, ref in enumerate((a_ref, b_ref)):
            copy = pltpu.make_async_copy(
                in_ref.at[slot, j], ref.at[pl.ds(i * BLOCK, BLOCK)], sems.at[i, j]
            )
            copy.start()
            copies.append(copy)
    for copy in copies:
        copy.wait()


def attend_kernel(clusters, table_ref, in_ref, out_ref, carry_ref, first_ref):
    scale = 1.0 / math.sqrt(DH)
    factor = scale * math.log2(math.e)

    def attend(c, following, have_part, own_count, near_count):
        own_src = [table_ref[1 + p, c] for p in range(own_count)]
        near_src = [table_ref[1 + p, following] for p in range(near_count)]
        sources = own_src + near_src
        keys = [in_ref[s, 0] for s in sources]
        vals = [in_ref[s, 1] for s in sources]
        q = jnp.concatenate(keys[:own_count], axis=0)
        g = jnp.concatenate([in_ref[s, 2] for s in own_src], axis=0)
        width = own_count * BLOCK
        ahead = lax.broadcasted_iota(jnp.int32, (BLOCK, width), 1) - lax.broadcasted_iota(
            jnp.int32, (BLOCK, width), 0
        )
        scores = [dot(k, q, NT) for k in keys]
        for p in range(own_count):
            scores[p] = jnp.where(ahead == p * BLOCK, -1e30, scores[p])
        top = functools.reduce(jnp.maximum, [jnp.max(s, axis=0, keepdims=True) for s in scores])
        weights = [jnp.exp2((s - top) * factor) for s in scores]
        dprobs = [dot(v, g, NT) for v in vals]
        total = sum(jnp.sum(w, axis=0, keepdims=True) for w in weights)
        inverse = 1.0 / total
        delta = (
            sum(jnp.sum(w * d, axis=0, keepdims=True) for w, d in zip(weights, dprobs)) * inverse
        )
        probs = [w * inverse for w in weights]
        dscores = [(p * (d - delta)).astype(jnp.bfloat16) for p, d in zip(probs, dprobs)]
        grad_w = [dot(p.astype(jnp.bfloat16), g, NN) for p in probs]
        grad_k = [dot(s, q, NN) for s in dscores]
        grad_q = dot(
            jnp.concatenate(dscores, axis=0), jnp.concatenate(keys, axis=0), TN
        )
        for p in range(own_count):
            own_qk = (grad_q[p * BLOCK : (p + 1) * BLOCK] + grad_k[p]) * scale
            own_v = grad_w[p]
            own_qk = own_qk + jnp.where(have_part, carry_ref[0, p], 0.0)
            own_v = own_v + jnp.where(have_part, carry_ref[1, p], 0.0)
            out_ref[own_src[p], 0] = own_qk.astype(jnp.bfloat16)
            out_ref[own_src[p], 1] = own_v.astype(jnp.bfloat16)

            @pl.when(c == 0)
            def _():
                first_ref[0, p] = own_qk
                first_ref[1, p] = own_v

        for p in range(near_count):
            carry_ref[0, p] = grad_k[own_count + p] * scale
            carry_ref[1, p] = grad_w[own_count + p]

    def step(c, have_part):
        following = lax.rem(c + 1, clusters)
        own = table_ref[0, c]
        near = jnp.where(table_ref[3, c] > 0, table_ref[0, following], 0)
        for own_count in (1, 2):
            for near_count in (0, 1, 2):

                @pl.when((own == own_count) & (near == near_count))
                def _():
                    attend(c, following, have_part > 0, own_count, near_count)

        return ((own > 0) & (near > 0)).astype(jnp.int32)

    have_part = lax.fori_loop(0, clusters, step, jnp.int32(0))
    for p in range(2):

        @pl.when((have_part > 0) & (table_ref[0, 0] > p))
        def _():
            source = table_ref[1 + p, 0]
            for j in range(2):
                out_ref[source, j] = (first_ref[j, p] + carry_ref[j, p]).astype(jnp.bfloat16)


def per_device(shared_qk, values, cotangent, cluster_ids, neighbour):
    n_seq = lax.axis_size("seq")
    seq_index = lax.axis_index("seq")
    tokens, lanes = shared_qk.shape
    per_source = tokens // BLOCK
    group_size = neighbour.shape[0] // n_seq
    any_space = pl.BlockSpec(memory_space=pl.ANY)
    smem = pl.BlockSpec(memory_space=pltpu.SMEM)
    vmem = pl.BlockSpec(memory_space=pltpu.VMEM)

    sent = pl.pallas_call(
        functools.partial(pack_kernel, per_source, group_size),
        out_shape=jax.ShapeDtypeStruct((n_seq, 3, BLOCK, lanes), shared_qk.dtype),
        in_specs=[smem, any_space, any_space, any_space],
        out_specs=vmem,
        scratch_shapes=[pltpu.SemaphoreType.DMA((per_source, 3))],
        name="pack",
    )(cluster_ids, shared_qk, values, cotangent)
    arrived = lax.all_to_all(sent, "seq", split_axis=0, concat_axis=0, tiled=True)

    local = seq_index * group_size + jnp.arange(group_size, dtype=jnp.int32)
    member = cluster_ids[None, :] == local[:, None]
    source = jnp.arange(cluster_ids.shape[0], dtype=jnp.int32)[None, :] // per_source
    table = jnp.stack(
        [
            jnp.sum(member.astype(jnp.int32), axis=1),
            jnp.min(jnp.where(member, source, n_seq - 1), axis=1),
            jnp.max(jnp.where(member, source, 0), axis=1),
            lax.dynamic_slice_in_dim(neighbour, seq_index * group_size, group_size) + 1,
        ]
    )
    returned = pl.pallas_call(
        functools.partial(attend_kernel, group_size),
        out_shape=jax.ShapeDtypeStruct((n_seq, 2, BLOCK, lanes), shared_qk.dtype),
        in_specs=[smem, vmem],
        out_specs=vmem,
        scratch_shapes=[
            pltpu.VMEM((2, 2, BLOCK, lanes), jnp.float32),
            pltpu.VMEM((2, 2, BLOCK, lanes), jnp.float32),
        ],
        compiler_params=pltpu.CompilerParams(vmem_limit_bytes=32 * 1024 * 1024),
        name="attend",
    )(table, arrived)
    home = lax.all_to_all(returned, "seq", split_axis=0, concat_axis=0, tiled=True)

    out = jax.ShapeDtypeStruct((tokens, lanes), shared_qk.dtype)
    return pl.pallas_call(
        functools.partial(unpack_kernel, per_source, group_size),
        out_shape=(out, out),
        in_specs=[smem, vmem],
        out_specs=(any_space, any_space),
        scratch_shapes=[pltpu.SemaphoreType.DMA((per_source, 2))],
        name="unpack",
    )(cluster_ids, home)


def solution(mesh):
    in_specs = (P("seq", "head"), P("seq", "head"), P("seq", "head"), P(), P())
    out_specs = (P("seq", "head"), P("seq", "head"))
    return jax.shard_map(
        per_device, mesh=mesh, in_specs=in_specs, out_specs=out_specs, check_vma=False
    )
```

```python
import functools
import math

import jax
import jax.numpy as jnp
from jax import lax
from jax.experimental import pallas as pl
from jax.experimental.pallas import tpu as pltpu
from jax.sharding import PartitionSpec as P

BLOCK = 128
DH = 128
NT = (((1,), (1,)), ((), ()))
NN = (((1,), (0,)), ((), ()))
TN = (((0,), (0,)), ((), ()))


def dot(a, b, dims):
    return lax.dot_general(a, b, dims, preferred_element_type=jnp.float32)


def blocks_of(rows):
    return [rows[i : i + BLOCK] for i in range(0, rows.shape[0], BLOCK)]


def pack_kernel(chunk, group_size, ids_ref, a_ref, b_ref, c_ref, out_ref, held, in_sems, out_sems):
    per_source = held.shape[0]
    base = lax.axis_index("seq") * per_source
    arriving, leaving = [], []
    for k in range(per_source // chunk):
        for j, ref in enumerate((a_ref, b_ref, c_ref)):
            blocks = pl.ds(k * chunk, chunk)
            copy = pltpu.make_async_copy(ref.at[blocks], held.at[blocks, j], in_sems.at[k, j])
            copy.start()
            arriving.append(copy)
    for k in range(per_source // chunk):
        for copy in arriving[3 * k : 3 * k + 3]:
            copy.wait()
        for i in range(k * chunk, (k + 1) * chunk):
            slot = lax.div(ids_ref[base + i], group_size)
            copy = pltpu.make_async_copy(held.at[i], out_ref.at[slot], out_sems.at[i])
            copy.start()
            leaving.append(copy)
    for copy in leaving:
        copy.wait()


def unpack_kernel(per_source, group_size, ids_ref, in_ref, a_ref, b_ref, sems):
    base = lax.axis_index("seq") * per_source
    copies = []
    for i in range(per_source):
        slot = ids_ref[base + i] // group_size
        for j, ref in enumerate((a_ref, b_ref)):
            copy = pltpu.make_async_copy(
                in_ref.at[slot, j], ref.at[pl.ds(i * BLOCK, BLOCK)], sems.at[i, j]
            )
            copy.start()
            copies.append(copy)
    for copy in copies:
        copy.wait()


def attend_kernel(clusters, lanes, table_ref, in_ref, out_ref, carry_ref, first_ref):
    scale = 1.0 / math.sqrt(DH)
    factor = scale * math.log2(math.e)
    length = clusters // lanes

    def following(c):
        return lax.rem(c + 1, clusters)

    def near_of(c):
        return jnp.where(table_ref[3, c] > 0, table_ref[0, following(c)], 0)

    def attend(c, have, lane, own_most, near_most):
        own, near = table_ref[0, c], near_of(c)
        own_src = [table_ref[1 + p, c] for p in range(own_most)]
        near_src = [table_ref[1 + p, following(c)] for p in range(near_most)]
        valid = [own > p for p in range(own_most)] + [near > p for p in range(near_most)]
        sources = own_src + near_src

        def load(which, p):
            block = in_ref[sources[p], which]
            return jnp.where(valid[p], block, jnp.zeros_like(block))

        count = own_most + near_most
        keys = [load(0, p) for p in range(count)]
        vals = [load(1, p) for p in range(count)]
        q = jnp.concatenate(keys[:own_most], axis=0)
        g = jnp.concatenate([load(2, p) for p in range(own_most)], axis=0)
        parts = [
            [jnp.where(have > p, carry_ref[lane, j, p], 0.0) for p in range(own_most)]
            for j in range(2)
        ]
        width = own_most * BLOCK
        ahead = lax.broadcasted_iota(jnp.int32, (BLOCK, width), 1) - lax.broadcasted_iota(
            jnp.int32, (BLOCK, width), 0
        )
        scores = blocks_of(dot(jnp.concatenate(keys, axis=0), q, NT))
        for p in range(count):
            if p < own_most:
                scores[p] = jnp.where(ahead == p * BLOCK, -1e30, scores[p])
            if p > 0:
                scores[p] = jnp.where(valid[p], scores[p], -1e30)
        top = functools.reduce(jnp.maximum, [jnp.max(s, axis=0, keepdims=True) for s in scores])
        weights = [jnp.exp2((s - top) * factor) for s in scores]
        dprobs = blocks_of(dot(jnp.concatenate(vals, axis=0), g, NT))
        total = sum(jnp.sum(w, axis=0, keepdims=True) for w in weights)
        inverse = 1.0 / total
        delta = (
            sum(jnp.sum(w * d, axis=0, keepdims=True) for w, d in zip(weights, dprobs)) * inverse
        )
        probs = [w * inverse for w in weights]
        dscores = [(p * (d - delta)).astype(jnp.bfloat16) for p, d in zip(probs, dprobs)]
        grad_w = blocks_of(dot(jnp.concatenate([p.astype(jnp.bfloat16) for p in probs], axis=0), g, NN))
        dscores = jnp.concatenate(dscores, axis=0)
        grad_k = blocks_of(dot(dscores, q, NN))
        grad_q = dot(dscores, jnp.concatenate(keys, axis=0), TN)
        own_grads = [
            (
                (grad_q[p * BLOCK : (p + 1) * BLOCK] + grad_k[p]) * scale + parts[0][p],
                grad_w[p] + parts[1][p],
            )
            for p in range(own_most)
        ]
        near_grads = [(grad_k[own_most + p] * scale, grad_w[own_most + p]) for p in range(near_most)]
        return own_src, own, own_grads, near_grads

    def attend_all(i, haves, own_most, near_most):
        results = [
            attend(i + lane * length, haves[lane], lane, own_most, near_most)
            for lane in range(lanes)
        ]
        for lane, (own_src, own, own_grads, near_grads) in enumerate(results):
            for p, grads in enumerate(near_grads):
                for j in range(2):
                    carry_ref[lane, j, p] = grads[j]
            for p, grads in enumerate(own_grads):

                @pl.when(own > p)
                def _():
                    for j in range(2):
                        out_ref[own_src[p], j] = grads[j].astype(jnp.bfloat16)

                @pl.when(i == 0)
                def _():
                    for j in range(2):
                        first_ref[lane, j, p] = grads[j]

    def step(i, haves):
        cs = [i + lane * length for lane in range(lanes)]
        owns = [table_ref[0, c] for c in cs]
        nears = [jnp.where(own > 0, near_of(c), 0) for own, c in zip(owns, cs)]
        own_top = functools.reduce(jnp.maximum, owns)
        near_top = functools.reduce(jnp.maximum, nears)
        for own_most in (1, 2):
            for near_most in (0, 1, 2):

                @pl.when((own_top == own_most) & (near_top == near_most))
                def _():
                    attend_all(i, haves, own_most, near_most)

        return tuple(nears)

    haves = lax.fori_loop(0, length, step, (jnp.int32(0),) * lanes)
    for lane in range(lanes):
        c = lane * length
        for p in range(2):

            @pl.when((haves[lane - 1] > p) & (table_ref[0, c] > p))
            def _():
                source = table_ref[1 + p, c]
                for j in range(2):
                    total = first_ref[lane, j, p] + carry_ref[(lane - 1) % lanes, j, p]
                    out_ref[source, j] = total.astype(jnp.bfloat16)


def per_device(shared_qk, values, cotangent, cluster_ids, neighbour):
    n_seq = lax.axis_size("seq")
    seq_index = lax.axis_index("seq")
    tokens, lanes = shared_qk.shape
    per_source = tokens // BLOCK
    group_size = neighbour.shape[0] // n_seq
    any_space = pl.BlockSpec(memory_space=pl.ANY)
    smem = pl.BlockSpec(memory_space=pltpu.SMEM)
    vmem = pl.BlockSpec(memory_space=pltpu.VMEM)

    sent = pl.pallas_call(
        functools.partial(pack_kernel, 4, group_size),
        out_shape=jax.ShapeDtypeStruct((n_seq, 3, BLOCK, lanes), shared_qk.dtype),
        in_specs=[smem, any_space, any_space, any_space],
        out_specs=any_space,
        scratch_shapes=[
            pltpu.VMEM((per_source, 3, BLOCK, lanes), shared_qk.dtype),
            pltpu.SemaphoreType.DMA((per_source // 4, 3)),
            pltpu.SemaphoreType.DMA((per_source,)),
        ],
        name="pack",
    )(cluster_ids, *(x.reshape(-1, BLOCK, lanes) for x in (shared_qk, values, cotangent)))
    arrived = lax.all_to_all(sent, "seq", split_axis=0, concat_axis=0, tiled=True)

    local = seq_index * group_size + jnp.arange(group_size, dtype=jnp.int32)
    member = cluster_ids[None, :] == local[:, None]
    source = jnp.arange(cluster_ids.shape[0], dtype=jnp.int32)[None, :] // per_source
    table = jnp.stack(
        [
            jnp.sum(member.astype(jnp.int32), axis=1),
            jnp.min(jnp.where(member, source, n_seq - 1), axis=1),
            jnp.max(jnp.where(member, source, 0), axis=1),
            lax.dynamic_slice_in_dim(neighbour, seq_index * group_size, group_size) + 1,
        ]
    )
    returned = pl.pallas_call(
        functools.partial(attend_kernel, group_size, 1),
        out_shape=jax.ShapeDtypeStruct((n_seq, 2, BLOCK, lanes), shared_qk.dtype),
        in_specs=[smem, vmem],
        out_specs=vmem,
        scratch_shapes=[
            pltpu.VMEM((2, 2, 2, BLOCK, lanes), jnp.float32),
            pltpu.VMEM((2, 2, 2, BLOCK, lanes), jnp.float32),
        ],
        compiler_params=pltpu.CompilerParams(vmem_limit_bytes=16 * 1024 * 1024),
        name="attend",
    )(table, arrived)
    home = lax.all_to_all(returned, "seq", split_axis=0, concat_axis=0, tiled=True)

    out = jax.ShapeDtypeStruct((tokens, lanes), shared_qk.dtype)
    return pl.pallas_call(
        functools.partial(unpack_kernel, per_source, group_size),
        out_shape=(out, out),
        in_specs=[smem, vmem],
        out_specs=(any_space, any_space),
        scratch_shapes=[pltpu.SemaphoreType.DMA((per_source, 2))],
        compiler_params=pltpu.CompilerParams(vmem_limit_bytes=8 * 1024 * 1024),
        name="unpack",
    )(cluster_ids, home)


def solution(mesh):
    in_specs = (P("seq", "head"), P("seq", "head"), P("seq", "head"), P(), P())
    out_specs = (P("seq", "head"), P("seq", "head"))
    return jax.shard_map(
        per_device, mesh=mesh, in_specs=in_specs, out_specs=out_specs, check_vma=False
    )
```

```python
import functools
import math

import jax
import jax.numpy as jnp
from jax import lax
from jax.experimental import pallas as pl
from jax.experimental.pallas import tpu as pltpu
from jax.sharding import PartitionSpec as P

BLOCK = 128
DH = 128
TOGETHER = (4, 4, 2, 2, 2, 2)
NT = (((1,), (1,)), ((), ()))
NN = (((1,), (0,)), ((), ()))
TN = (((0,), (0,)), ((), ()))


def dot(a, b, dims):
    return lax.dot_general(a, b, dims, preferred_element_type=jnp.float32)


def pack_kernel(chunk, group_size, ids_ref, a_ref, b_ref, c_ref, out_ref, held, in_sems, out_sems):
    per_source = held.shape[0]
    base = lax.axis_index("seq") * per_source
    arriving, leaving = [], []
    for k in range(per_source // chunk):
        for j, ref in enumerate((a_ref, b_ref, c_ref)):
            blocks = pl.ds(k * chunk, chunk)
            copy = pltpu.make_async_copy(ref.at[blocks], held.at[blocks, j], in_sems.at[k, j])
            copy.start()
            arriving.append(copy)
    for k in range(per_source // chunk):
        for copy in arriving[3 * k : 3 * k + 3]:
            copy.wait()
        for i in range(k * chunk, (k + 1) * chunk):
            slot = lax.div(ids_ref[base + i], group_size)
            copy = pltpu.make_async_copy(held.at[i], out_ref.at[slot], out_sems.at[i])
            copy.start()
            leaving.append(copy)
    for copy in leaving:
        copy.wait()


def unpack_kernel(per_source, group_size, ids_ref, in_ref, a_ref, b_ref, sems):
    base = lax.axis_index("seq") * per_source
    copies = []
    for i in range(per_source):
        slot = ids_ref[base + i] // group_size
        for j, ref in enumerate((a_ref, b_ref)):
            copy = pltpu.make_async_copy(
                in_ref.at[slot, j], ref.at[pl.ds(i * BLOCK, BLOCK)], sems.at[i, j]
            )
            copy.start()
            copies.append(copy)
    for copy in copies:
        copy.wait()


def attend_kernel(clusters, together, table_ref, in_ref, out_ref, own_ref, part_ref):
    scale = 1.0 / math.sqrt(DH)
    factor = scale * math.log2(math.e)

    def attend(cs, own_count, near_count):
        lanes = range(len(cs))
        own_src = [[table_ref[1 + p, c] for p in range(own_count)] for c in cs]
        near_src = [
            [table_ref[1 + p, lax.rem(c + 1, clusters)] for p in range(near_count)] for c in cs
        ]

        def load(which, sources):
            return jnp.concatenate([in_ref[s, which] for s in sources], axis=0)

        k = [load(0, own_src[i] + near_src[i]) for i in lanes]
        w = [load(1, own_src[i] + near_src[i]) for i in lanes]
        g = [load(2, own_src[i]) for i in lanes]
        width = own_count * BLOCK
        q = [x[:width] for x in k]
        ahead = lax.broadcasted_iota(jnp.int32, (width, width), 1) - lax.broadcasted_iota(
            jnp.int32, (width, width), 0
        )
        scores = [dot(k[i], q[i], NT) for i in lanes]
        dprobs = [dot(w[i], g[i], NT) for i in lanes]
        own_scores = [jnp.where(ahead == 0, -1e30, x[:width]) for x in scores]
        if near_count:
            scores = [jnp.concatenate([own_scores[i], scores[i][width:]], axis=0) for i in lanes]
        else:
            scores = own_scores
        top = [jnp.max(x, axis=0, keepdims=True) for x in scores]
        weights = [jnp.exp2((scores[i] - top[i]) * factor) for i in lanes]
        inverse = [1.0 / jnp.sum(x, axis=0, keepdims=True) for x in weights]
        delta = [
            jnp.sum(weights[i] * dprobs[i], axis=0, keepdims=True) * inverse[i] for i in lanes
        ]
        probs = [weights[i] * inverse[i] for i in lanes]
        dscores = [(probs[i] * (dprobs[i] - delta[i])).astype(jnp.bfloat16) for i in lanes]
        grad_q = [dot(dscores[i], k[i], TN) for i in lanes]
        grad_w = [dot(probs[i].astype(jnp.bfloat16), g[i], NN) for i in lanes]
        grad_k = [dot(dscores[i], q[i], NN) for i in lanes]
        for i in lanes:
            for p in range(own_count):
                rows = slice(p * BLOCK, (p + 1) * BLOCK)
                own_ref[0, own_src[i][p]] = (grad_q[i][rows] + grad_k[i][rows]) * scale
                own_ref[1, own_src[i][p]] = grad_w[i][rows]
            for p in range(near_count):
                rows = slice(width + p * BLOCK, width + (p + 1) * BLOCK)
                part_ref[0, near_src[i][p]] = grad_k[i][rows] * scale
                part_ref[1, near_src[i][p]] = grad_w[i][rows]

    for own_count in (1, 2):
        for near_count in (0, 1, 2):
            shape = 3 * own_count + near_count
            first, end = table_ref[6, shape], table_ref[6, shape + 1]
            lanes = together[shape - 3]

            @pl.loop(0, lax.div(end - first + (lanes - 1), lanes))
            def _(turn):
                at = [jnp.minimum(first + turn * lanes + i, end - 1) for i in range(lanes)]
                attend([table_ref[5, a] for a in at], own_count, near_count)

    @pl.loop(0, clusters, unroll=True)
    def _(c):
        for p in range(2):
            source = table_ref[1 + p, c]

            @pl.when(table_ref[0, c] > p)
            def _():
                for j in range(2):
                    part = jnp.where(table_ref[4, c] > p, part_ref[j, source], 0.0)
                    out_ref[source, j] = (own_ref[j, source] + part).astype(jnp.bfloat16)


def per_device(shared_qk, values, cotangent, cluster_ids, neighbour):
    n_seq = lax.axis_size("seq")
    seq_index = lax.axis_index("seq")
    tokens, lanes = shared_qk.shape
    per_source = tokens // BLOCK
    group_size = neighbour.shape[0] // n_seq
    any_space = pl.BlockSpec(memory_space=pl.ANY)
    smem = pl.BlockSpec(memory_space=pltpu.SMEM)
    vmem = pl.BlockSpec(memory_space=pltpu.VMEM)

    sent = pl.pallas_call(
        functools.partial(pack_kernel, 4, group_size),
        out_shape=jax.ShapeDtypeStruct((n_seq, 3, BLOCK, lanes), shared_qk.dtype),
        in_specs=[smem, any_space, any_space, any_space],
        out_specs=any_space,
        scratch_shapes=[
            pltpu.VMEM((per_source, 3, BLOCK, lanes), shared_qk.dtype),
            pltpu.SemaphoreType.DMA((per_source // 4, 3)),
            pltpu.SemaphoreType.DMA((per_source,)),
        ],
        name="pack",
    )(cluster_ids, *(x.reshape(-1, BLOCK, lanes) for x in (shared_qk, values, cotangent)))
    arrived = lax.all_to_all(sent, "seq", split_axis=0, concat_axis=0, tiled=True)

    local = seq_index * group_size + jnp.arange(group_size, dtype=jnp.int32)
    member = cluster_ids[None, :] == local[:, None]
    source = jnp.arange(cluster_ids.shape[0], dtype=jnp.int32)[None, :] // per_source
    held = jnp.sum(member.astype(jnp.int32), axis=1)
    flagged = lax.dynamic_slice_in_dim(neighbour, seq_index * group_size, group_size) >= 0
    near = jnp.where(flagged & (held > 0), jnp.roll(held, -1), 0)
    shape = 3 * held + near
    ids = jnp.arange(group_size, dtype=jnp.int32)
    before = (shape[None, :] < shape[:, None]) | (
        (shape[None, :] == shape[:, None]) & (ids[None, :] < ids[:, None])
    )
    rank = jnp.sum(before.astype(jnp.int32), axis=1)
    order = jnp.sum(jnp.where(rank[None, :] == ids[:, None], ids[None, :], 0), axis=1)
    starts = jnp.sum((shape[None, :] < ids[:, None]).astype(jnp.int32), axis=1)
    table = jnp.stack(
        [
            held,
            jnp.min(jnp.where(member, source, n_seq - 1), axis=1),
            jnp.max(jnp.where(member, source, 0), axis=1),
            near,
            jnp.roll(near, 1),
            order,
            starts,
        ]
    )
    returned = pl.pallas_call(
        functools.partial(attend_kernel, group_size, TOGETHER),
        out_shape=jax.ShapeDtypeStruct((n_seq, 2, BLOCK, lanes), shared_qk.dtype),
        in_specs=[smem, vmem],
        out_specs=vmem,
        scratch_shapes=[
            pltpu.VMEM((2, n_seq, BLOCK, lanes), jnp.float32),
            pltpu.VMEM((2, n_seq, BLOCK, lanes), jnp.float32),
        ],
        compiler_params=pltpu.CompilerParams(vmem_limit_bytes=32 * 1024 * 1024),
        name="attend",
    )(table, arrived)
    home = lax.all_to_all(returned, "seq", split_axis=0, concat_axis=0, tiled=True)

    out = jax.ShapeDtypeStruct((tokens, lanes), shared_qk.dtype)
    return pl.pallas_call(
        functools.partial(unpack_kernel, per_source, group_size),
        out_shape=(out, out),
        in_specs=[smem, vmem],
        out_specs=(any_space, any_space),
        scratch_shapes=[pltpu.SemaphoreType.DMA((per_source, 2))],
        compiler_params=pltpu.CompilerParams(vmem_limit_bytes=8 * 1024 * 1024),
        name="unpack",
    )(cluster_ids, home)


def solution(mesh):
    in_specs = (P("seq", "head"), P("seq", "head"), P("seq", "head"), P(), P())
    out_specs = (P("seq", "head"), P("seq", "head"))
    return jax.shard_map(
        per_device, mesh=mesh, in_specs=in_specs, out_specs=out_specs, check_vma=False
    )
```

```python
import functools
import math

import jax
import jax.numpy as jnp
from jax import lax
from jax.experimental import pallas as pl
from jax.experimental.pallas import tpu as pltpu
from jax.sharding import PartitionSpec as P

BLOCK = 128
DH = 128
TOGETHER = (4, 4, 2, 2, 2, 2)
PACK, UNPACK = 8, 8
NT = (((1,), (1,)), ((), ()))
NN = (((1,), (0,)), ((), ()))
TN = (((0,), (0,)), ((), ()))


def dot(a, b, dims):
    return lax.dot_general(a, b, dims, preferred_element_type=jnp.float32)


def make_table(ids, neighbour, group_size, per_source, n_seq, table_ref):
    total = ids.shape[1]
    member_of = lax.broadcasted_iota(jnp.int32, (group_size, total), 0)
    local = member_of + lax.axis_index("seq") * group_size
    lane = lax.broadcasted_iota(jnp.int32, (group_size, total), 1)
    member = ids == local
    source = lax.div(lane, per_source)

    def count(mask):
        return jnp.sum(jnp.where(mask, 1, 0), axis=1, keepdims=True)

    held = count(member)
    low = jnp.min(jnp.where(member, source, n_seq - 1), axis=1, keepdims=True)
    high = jnp.max(jnp.where(member, source, 0), axis=1, keepdims=True)
    flagged = count((lane == local) & (neighbour >= 0))
    i = lax.broadcasted_iota(jnp.int32, (group_size, group_size), 0)
    j = lax.broadcasted_iota(jnp.int32, (group_size, group_size), 1)

    def as_row(column):
        return jnp.sum(jnp.where(i == j, column, 0), axis=0, keepdims=True)

    def picked(row, mask):
        return jnp.sum(jnp.where(mask, row, 0), axis=1, keepdims=True)

    following = picked(as_row(held), j == lax.rem(i + 1, group_size))
    near = jnp.where((flagged > 0) & (held > 0), following, 0)
    part = picked(as_row(near), j == lax.rem(i + (group_size - 1), group_size))
    shape = 3 * held + near
    shape_row = as_row(shape)
    rank = count((shape_row < shape) | ((shape_row == shape) & (j < i)))
    order = picked(j, as_row(rank) == i)
    starts = count(shape_row < i)
    place = lax.broadcasted_iota(jnp.int32, table_ref.shape, 1)
    table = jnp.zeros(table_ref.shape, jnp.int32)
    for k, column in enumerate((held, low, high, near, part, order, starts)):
        table = jnp.where(place == k, column, table)
    table_ref[...] = table


def pack_kernel(
    chunk,
    group_size,
    ids_ref,
    row_ref,
    near_ref,
    a_ref,
    b_ref,
    c_ref,
    out_ref,
    table_ref,
    ids,
    row,
    near,
    table,
    held,
    small_sems,
    in_sems,
    out_sems,
):
    per_source = held.shape[0]
    base = lax.axis_index("seq") * per_source
    small = [
        pltpu.make_async_copy(ref, scratch, small_sems.at[k])
        for k, (ref, scratch) in enumerate(((ids_ref, ids), (row_ref, row), (near_ref, near)))
    ]
    for copy in small:
        copy.start()
    arriving, leaving = [], []
    for k in range(per_source // chunk):
        for j, ref in enumerate((a_ref, b_ref, c_ref)):
            blocks = pl.ds(k * chunk, chunk)
            copy = pltpu.make_async_copy(ref.at[blocks], held.at[blocks, j], in_sems.at[k, j])
            copy.start()
            arriving.append(copy)
    for copy in small:
        copy.wait()
    slots = [lax.div(ids[base + i], group_size) for i in range(per_source)]
    for k in range(per_source // chunk):
        for copy in arriving[3 * k : 3 * k + 3]:
            copy.wait()
        for i in range(k * chunk, (k + 1) * chunk):
            copy = pltpu.make_async_copy(held.at[i], out_ref.at[slots[i]], out_sems.at[i])
            copy.start()
            leaving.append(copy)
    make_table(row[...], near[...], group_size, per_source, out_ref.shape[0], table)
    tabled = pltpu.make_async_copy(table, table_ref, small_sems.at[3])
    tabled.start()
    tabled.wait()
    for copy in leaving:
        copy.wait()


def unpack_kernel(chunk, group_size, ids_ref, in_ref, a_ref, b_ref, held, sems):
    per_source = held.shape[1]
    base = lax.axis_index("seq") * per_source
    leaving = []
    for k in range(per_source // chunk):
        for j, ref in enumerate((a_ref, b_ref)):
            for i in range(k * chunk, (k + 1) * chunk):
                held[j, i] = in_ref[lax.div(ids_ref[base + i], group_size), j]
            blocks = pl.ds(k * chunk, chunk)
            copy = pltpu.make_async_copy(held.at[j, blocks], ref.at[blocks], sems.at[k, j])
            copy.start()
            leaving.append(copy)
    for copy in leaving:
        copy.wait()


def attend_kernel(clusters, together, table_ref, in_ref, out_ref, own_ref, part_ref):
    scale = 1.0 / math.sqrt(DH)
    factor = scale * math.log2(math.e)

    def attend(cs, own_count, near_count):
        lanes = range(len(cs))
        own_src = [[table_ref[c, 1 + p] for p in range(own_count)] for c in cs]
        near_src = [
            [table_ref[lax.rem(c + 1, clusters), 1 + p] for p in range(near_count)] for c in cs
        ]

        def load(which, sources):
            return jnp.concatenate([in_ref[s, which] for s in sources], axis=0)

        k = [load(0, own_src[i] + near_src[i]) for i in lanes]
        w = [load(1, own_src[i] + near_src[i]) for i in lanes]
        g = [load(2, own_src[i]) for i in lanes]
        width = own_count * BLOCK
        q = [x[:width] for x in k]
        ahead = lax.broadcasted_iota(jnp.int32, (width, width), 1) - lax.broadcasted_iota(
            jnp.int32, (width, width), 0
        )
        scores = [dot(k[i], q[i], NT) for i in lanes]
        dprobs = [dot(w[i], g[i], NT) for i in lanes]
        own_scores = [jnp.where(ahead == 0, -1e30, x[:width]) for x in scores]
        if near_count:
            scores = [jnp.concatenate([own_scores[i], scores[i][width:]], axis=0) for i in lanes]
        else:
            scores = own_scores
        top = [jnp.max(x, axis=0, keepdims=True) for x in scores]
        weights = [jnp.exp2((scores[i] - top[i]) * factor) for i in lanes]
        inverse = [1.0 / jnp.sum(x, axis=0, keepdims=True) for x in weights]
        delta = [
            jnp.sum(weights[i] * dprobs[i], axis=0, keepdims=True) * inverse[i] for i in lanes
        ]
        probs = [weights[i] * inverse[i] for i in lanes]
        dscores = [(probs[i] * (dprobs[i] - delta[i])).astype(jnp.bfloat16) for i in lanes]
        grad_q = [dot(dscores[i], k[i], TN) for i in lanes]
        grad_w = [dot(probs[i].astype(jnp.bfloat16), g[i], NN) for i in lanes]
        grad_k = [dot(dscores[i], q[i], NN) for i in lanes]
        for i in lanes:
            for p in range(own_count):
                rows = slice(p * BLOCK, (p + 1) * BLOCK)
                own_ref[0, own_src[i][p]] = (grad_q[i][rows] + grad_k[i][rows]) * scale
                own_ref[1, own_src[i][p]] = grad_w[i][rows]
            for p in range(near_count):
                rows = slice(width + p * BLOCK, width + (p + 1) * BLOCK)
                part_ref[0, near_src[i][p]] = grad_k[i][rows] * scale
                part_ref[1, near_src[i][p]] = grad_w[i][rows]

    for own_count in (1, 2):
        for near_count in (0, 1, 2):
            shape = 3 * own_count + near_count
            first, end = table_ref[shape, 6], table_ref[shape + 1, 6]
            lanes = together[shape - 3]

            @pl.loop(0, lax.div(end - first + (lanes - 1), lanes))
            def _(turn):
                at = [jnp.minimum(first + turn * lanes + i, end - 1) for i in range(lanes)]
                attend([table_ref[a, 5] for a in at], own_count, near_count)

    @pl.loop(0, clusters, unroll=True)
    def _(c):
        for p in range(2):
            source = table_ref[c, 1 + p]

            @pl.when(table_ref[c, 0] > p)
            def _():
                for j in range(2):
                    part = jnp.where(table_ref[c, 4] > p, part_ref[j, source], 0.0)
                    out_ref[source, j] = (own_ref[j, source] + part).astype(jnp.bfloat16)


def per_device(shared_qk, values, cotangent, cluster_ids, neighbour):
    n_seq = lax.axis_size("seq")
    tokens, lanes = shared_qk.shape
    per_source = tokens // BLOCK
    group_size = neighbour.shape[0] // n_seq
    dtype = shared_qk.dtype
    any_space = pl.BlockSpec(memory_space=pl.ANY)
    smem = pl.BlockSpec(memory_space=pltpu.SMEM)
    vmem = pl.BlockSpec(memory_space=pltpu.VMEM)

    sent, table = pl.pallas_call(
        functools.partial(pack_kernel, PACK, group_size),
        out_shape=(
            jax.ShapeDtypeStruct((n_seq, 3, BLOCK, lanes), dtype),
            jax.ShapeDtypeStruct((group_size, 128), jnp.int32),
        ),
        in_specs=[any_space] * 6,
        out_specs=(any_space, any_space),
        scratch_shapes=[
            pltpu.SMEM(cluster_ids.shape, jnp.int32),
            pltpu.VMEM((1, cluster_ids.shape[0]), jnp.int32),
            pltpu.VMEM((1, neighbour.shape[0]), jnp.int32),
            pltpu.VMEM((group_size, 128), jnp.int32),
            pltpu.VMEM((per_source, 3, BLOCK, lanes), dtype),
            pltpu.SemaphoreType.DMA((4,)),
            pltpu.SemaphoreType.DMA((per_source // PACK, 3)),
            pltpu.SemaphoreType.DMA((per_source,)),
        ],
        name="pack",
    )(
        cluster_ids,
        cluster_ids.reshape(1, -1),
        neighbour.reshape(1, -1),
        *(x.reshape(-1, BLOCK, lanes) for x in (shared_qk, values, cotangent)),
    )
    arrived = lax.all_to_all(sent, "seq", split_axis=0, concat_axis=0, tiled=True)

    returned = pl.pallas_call(
        functools.partial(attend_kernel, group_size, TOGETHER),
        out_shape=jax.ShapeDtypeStruct((n_seq, 2, BLOCK, lanes), dtype),
        in_specs=[smem, vmem],
        out_specs=vmem,
        scratch_shapes=[
            pltpu.VMEM((2, n_seq, BLOCK, lanes), jnp.float32),
            pltpu.VMEM((2, n_seq, BLOCK, lanes), jnp.float32),
        ],
        compiler_params=pltpu.CompilerParams(vmem_limit_bytes=32 * 1024 * 1024),
        name="attend",
    )(table, arrived)
    home = lax.all_to_all(returned, "seq", split_axis=0, concat_axis=0, tiled=True)

    out = jax.ShapeDtypeStruct((per_source, BLOCK, lanes), dtype)
    grads = pl.pallas_call(
        functools.partial(unpack_kernel, UNPACK, group_size),
        out_shape=(out, out),
        in_specs=[smem, vmem],
        out_specs=(any_space, any_space),
        scratch_shapes=[
            pltpu.VMEM((2, per_source, BLOCK, lanes), dtype),
            pltpu.SemaphoreType.DMA((per_source // UNPACK, 2)),
        ],
        compiler_params=pltpu.CompilerParams(vmem_limit_bytes=8 * 1024 * 1024),
        name="unpack",
    )(cluster_ids, home)
    return tuple(x.reshape(tokens, lanes) for x in grads)


def solution(mesh):
    in_specs = (P("seq", "head"), P("seq", "head"), P("seq", "head"), P(), P())
    out_specs = (P("seq", "head"), P("seq", "head"))
    return jax.shard_map(
        per_device, mesh=mesh, in_specs=in_specs, out_specs=out_specs, check_vma=False
    )
```

```python
import functools
import math

import jax
import jax.numpy as jnp
from jax import lax
from jax.experimental import pallas as pl
from jax.experimental.pallas import tpu as pltpu
from jax.sharding import PartitionSpec as P

BLOCK = 128
DH = 128
TOGETHER = (4, 4, 2, 2, 2, 2)
PACK, UNPACK = 8, 8
NT = (((1,), (1,)), ((), ()))
NN = (((1,), (0,)), ((), ()))
TN = (((0,), (0,)), ((), ()))


def dot(a, b, dims):
    return lax.dot_general(a, b, dims, preferred_element_type=jnp.float32)


def make_table(ids, neighbour, group_size, per_source, n_seq, table_ref):
    total = ids.shape[1]
    member_of = lax.broadcasted_iota(jnp.int32, (group_size, total), 0)
    local = member_of + lax.axis_index("seq") * group_size
    lane = lax.broadcasted_iota(jnp.int32, (group_size, total), 1)
    member = ids == local
    source = lax.div(lane, per_source)

    def count(mask):
        return jnp.sum(jnp.where(mask, 1, 0), axis=1, keepdims=True)

    held = count(member)
    low = jnp.min(jnp.where(member, source, n_seq - 1), axis=1, keepdims=True)
    high = jnp.max(jnp.where(member, source, 0), axis=1, keepdims=True)
    flagged = count((lane == local) & (neighbour >= 0))
    i = lax.broadcasted_iota(jnp.int32, (group_size, group_size), 0)
    j = lax.broadcasted_iota(jnp.int32, (group_size, group_size), 1)

    def as_row(column):
        return jnp.sum(jnp.where(i == j, column, 0), axis=0, keepdims=True)

    def picked(row, mask):
        return jnp.sum(jnp.where(mask, row, 0), axis=1, keepdims=True)

    following = picked(as_row(held), j == lax.rem(i + 1, group_size))
    near = jnp.where((flagged > 0) & (held > 0), following, 0)
    part = picked(as_row(near), j == lax.rem(i + (group_size - 1), group_size))
    shape = 3 * held + near
    shape_row = as_row(shape)
    rank = count((shape_row < shape) | ((shape_row == shape) & (j < i)))
    order = picked(j, as_row(rank) == i)
    starts = count(shape_row < i)
    place = lax.broadcasted_iota(jnp.int32, table_ref.shape, 1)
    table = jnp.zeros(table_ref.shape, jnp.int32)
    for k, column in enumerate((held, low, high, near, part, order, starts)):
        table = jnp.where(place == k, column, table)
    table_ref[...] = table


def pack_kernel(
    chunk,
    group_size,
    ids_ref,
    row_ref,
    near_ref,
    a_ref,
    b_ref,
    c_ref,
    out_ref,
    table_ref,
    ids,
    row,
    near,
    table,
    held,
    small_sems,
    in_sems,
    out_sems,
):
    per_source = held.shape[0]
    base = lax.axis_index("seq") * per_source
    small = [
        pltpu.make_async_copy(ref, scratch, small_sems.at[k])
        for k, (ref, scratch) in enumerate(((ids_ref, ids), (row_ref, row), (near_ref, near)))
    ]
    for copy in small:
        copy.start()
    arriving, leaving = [], []
    for k in range(per_source // chunk):
        for j, ref in enumerate((a_ref, b_ref, c_ref)):
            blocks = pl.ds(k * chunk, chunk)
            copy = pltpu.make_async_copy(ref.at[blocks], held.at[blocks, j], in_sems.at[k, j])
            copy.start()
            arriving.append(copy)
    for copy in small:
        copy.wait()
    slots = [lax.div(ids[base + i], group_size) for i in range(per_source)]
    for k in range(per_source // chunk):
        for copy in arriving[3 * k : 3 * k + 3]:
            copy.wait()
        for i in range(k * chunk, (k + 1) * chunk):
            copy = pltpu.make_async_copy(held.at[i], out_ref.at[slots[i]], out_sems.at[i])
            copy.start()
            leaving.append(copy)
    make_table(row[...], near[...], group_size, per_source, out_ref.shape[0], table)
    tabled = pltpu.make_async_copy(table, table_ref, small_sems.at[3])
    tabled.start()
    tabled.wait()
    for copy in leaving:
        copy.wait()


def unpack_kernel(chunk, group_size, ids_ref, in_ref, a_ref, b_ref, held, sems):
    per_source = held.shape[1]
    base = lax.axis_index("seq") * per_source
    leaving = []
    for k in range(per_source // chunk):
        for j, ref in enumerate((a_ref, b_ref)):
            for i in range(k * chunk, (k + 1) * chunk):
                held[j, i] = in_ref[lax.div(ids_ref[base + i], group_size), j]
            blocks = pl.ds(k * chunk, chunk)
            copy = pltpu.make_async_copy(held.at[j, blocks], ref.at[blocks], sems.at[k, j])
            copy.start()
            leaving.append(copy)
    for copy in leaving:
        copy.wait()


def attend_kernel(clusters, together, table_ref, in_ref, out_ref, own_ref, part_ref):
    scale = 1.0 / math.sqrt(DH)
    factor = scale * math.log2(math.e)

    def attend(cs, own_count, near_count):
        lanes = range(len(cs))
        own_src = [[table_ref[c, 1 + p] for p in range(own_count)] for c in cs]
        near_src = [
            [table_ref[lax.rem(c + 1, clusters), 1 + p] for p in range(near_count)] for c in cs
        ]

        def load(which, sources):
            return jnp.concatenate([in_ref[s, which] for s in sources], axis=0)

        k = [load(0, own_src[i] + near_src[i]) for i in lanes]
        w = [load(1, own_src[i] + near_src[i]) for i in lanes]
        g = [load(2, own_src[i]) for i in lanes]
        width = own_count * BLOCK
        q = [x[:width] for x in k]
        ahead = lax.broadcasted_iota(jnp.int32, (width, width), 1) - lax.broadcasted_iota(
            jnp.int32, (width, width), 0
        )
        scores = [dot(k[i], q[i], NT) for i in lanes]
        dprobs = [dot(w[i], g[i], NT) for i in lanes]
        own_scores = [jnp.where(ahead == 0, -1e30, x[:width]) for x in scores]
        if near_count:
            scores = [jnp.concatenate([own_scores[i], scores[i][width:]], axis=0) for i in lanes]
        else:
            scores = own_scores
        top = [jnp.max(x, axis=0, keepdims=True) for x in scores]
        weights = [jnp.exp2((scores[i] - top[i]) * factor) for i in lanes]
        inverse = [1.0 / jnp.sum(x, axis=0, keepdims=True) for x in weights]
        delta = [
            jnp.sum(weights[i] * dprobs[i], axis=0, keepdims=True) * inverse[i] for i in lanes
        ]
        probs = [weights[i] * inverse[i] for i in lanes]
        dscores = [(probs[i] * (dprobs[i] - delta[i])).astype(jnp.bfloat16) for i in lanes]
        grad_w = [dot(probs[i].astype(jnp.bfloat16), g[i], NN) for i in lanes]
        grad_k = [dot(dscores[i], q[i], NN) for i in lanes]
        grad_q = [dot(dscores[i], k[i], TN) for i in lanes]
        for i in lanes:
            for p in range(own_count):
                rows = slice(p * BLOCK, (p + 1) * BLOCK)
                own_ref[0, own_src[i][p]] = (grad_q[i][rows] + grad_k[i][rows]) * scale
                own_ref[1, own_src[i][p]] = grad_w[i][rows]
            for p in range(near_count):
                rows = slice(width + p * BLOCK, width + (p + 1) * BLOCK)
                part_ref[0, near_src[i][p]] = grad_k[i][rows] * scale
                part_ref[1, near_src[i][p]] = grad_w[i][rows]

    for own_count in (1, 2):
        for near_count in (0, 1, 2):
            shape = 3 * own_count + near_count
            first, end = table_ref[shape, 6], table_ref[shape + 1, 6]
            lanes = together[shape - 3]

            whole = lax.div(end - first, lanes)
            rest = end - first - whole * lanes

            @pl.loop(0, whole + (rest > 1).astype(jnp.int32))
            def _(turn):
                at = [jnp.minimum(first + turn * lanes + i, end - 1) for i in range(lanes)]
                attend([table_ref[a, 5] for a in at], own_count, near_count)

            @pl.when(rest == 1)
            def _():
                attend([table_ref[end - 1, 5]], own_count, near_count)

    @pl.loop(0, clusters, unroll=True)
    def _(c):
        for p in range(2):
            source = table_ref[c, 1 + p]

            @pl.when(table_ref[c, 0] > p)
            def _():
                for j in range(2):
                    part = jnp.where(table_ref[c, 4] > p, part_ref[j, source], 0.0)
                    out_ref[source, j] = (own_ref[j, source] + part).astype(jnp.bfloat16)


def per_device(shared_qk, values, cotangent, cluster_ids, neighbour):
    n_seq = lax.axis_size("seq")
    tokens, lanes = shared_qk.shape
    per_source = tokens // BLOCK
    group_size = neighbour.shape[0] // n_seq
    dtype = shared_qk.dtype
    any_space = pl.BlockSpec(memory_space=pl.ANY)
    smem = pl.BlockSpec(memory_space=pltpu.SMEM)
    vmem = pl.BlockSpec(memory_space=pltpu.VMEM)

    sent, table = pl.pallas_call(
        functools.partial(pack_kernel, PACK, group_size),
        out_shape=(
            jax.ShapeDtypeStruct((n_seq, 3, BLOCK, lanes), dtype),
            jax.ShapeDtypeStruct((group_size, 128), jnp.int32),
        ),
        in_specs=[any_space] * 6,
        out_specs=(any_space, any_space),
        scratch_shapes=[
            pltpu.SMEM(cluster_ids.shape, jnp.int32),
            pltpu.VMEM((1, cluster_ids.shape[0]), jnp.int32),
            pltpu.VMEM((1, neighbour.shape[0]), jnp.int32),
            pltpu.VMEM((group_size, 128), jnp.int32),
            pltpu.VMEM((per_source, 3, BLOCK, lanes), dtype),
            pltpu.SemaphoreType.DMA((4,)),
            pltpu.SemaphoreType.DMA((per_source // PACK, 3)),
            pltpu.SemaphoreType.DMA((per_source,)),
        ],
        name="pack",
    )(
        cluster_ids,
        cluster_ids.reshape(1, -1),
        neighbour.reshape(1, -1),
        *(x.reshape(-1, BLOCK, lanes) for x in (shared_qk, values, cotangent)),
    )
    arrived = lax.all_to_all(sent, "seq", split_axis=0, concat_axis=0, tiled=True)

    returned = pl.pallas_call(
        functools.partial(attend_kernel, group_size, TOGETHER),
        out_shape=jax.ShapeDtypeStruct((n_seq, 2, BLOCK, lanes), dtype),
        in_specs=[smem, vmem],
        out_specs=vmem,
        scratch_shapes=[
            pltpu.VMEM((2, n_seq, BLOCK, lanes), jnp.float32),
            pltpu.VMEM((2, n_seq, BLOCK, lanes), jnp.float32),
        ],
        compiler_params=pltpu.CompilerParams(vmem_limit_bytes=32 * 1024 * 1024),
        name="attend",
    )(table, arrived)
    home = lax.all_to_all(returned, "seq", split_axis=0, concat_axis=0, tiled=True)

    out = jax.ShapeDtypeStruct((per_source, BLOCK, lanes), dtype)
    grads = pl.pallas_call(
        functools.partial(unpack_kernel, UNPACK, group_size),
        out_shape=(out, out),
        in_specs=[smem, vmem],
        out_specs=(any_space, any_space),
        scratch_shapes=[
            pltpu.VMEM((2, per_source, BLOCK, lanes), dtype),
            pltpu.SemaphoreType.DMA((per_source // UNPACK, 2)),
        ],
        compiler_params=pltpu.CompilerParams(vmem_limit_bytes=8 * 1024 * 1024),
        name="unpack",
    )(cluster_ids, home)
    return tuple(x.reshape(tokens, lanes) for x in grads)


def solution(mesh):
    in_specs = (P("seq", "head"), P("seq", "head"), P("seq", "head"), P(), P())
    out_specs = (P("seq", "head"), P("seq", "head"))
    return jax.shard_map(
        per_device, mesh=mesh, in_specs=in_specs, out_specs=out_specs, check_vma=False
    )
```

```python
import functools
import math

import jax
import jax.numpy as jnp
from jax import lax
from jax.experimental import pallas as pl
from jax.experimental.pallas import tpu as pltpu
from jax.sharding import PartitionSpec as P

BLOCK = 128
DH = 128
TOGETHER = (4, 4, 2, 2, 2, 2)
PACK, UNPACK = 8, 8
NT = (((1,), (1,)), ((), ()))
NN = (((1,), (0,)), ((), ()))
TN = (((0,), (0,)), ((), ()))


def dot(a, b, dims):
    return lax.dot_general(a, b, dims, preferred_element_type=jnp.float32)


def make_table(ids, neighbour, group_size, per_source, n_seq, table_ref):
    total = ids.shape[1]
    member_of = lax.broadcasted_iota(jnp.int32, (group_size, total), 0)
    local = member_of + lax.axis_index("seq") * group_size
    lane = lax.broadcasted_iota(jnp.int32, (group_size, total), 1)
    member = ids == local
    source = lax.div(lane, per_source)

    def count(mask):
        return jnp.sum(jnp.where(mask, 1, 0), axis=1, keepdims=True)

    held = count(member)
    low = jnp.min(jnp.where(member, source, n_seq - 1), axis=1, keepdims=True)
    high = jnp.max(jnp.where(member, source, 0), axis=1, keepdims=True)
    flagged = count((lane == local) & (neighbour >= 0))
    i = lax.broadcasted_iota(jnp.int32, (group_size, group_size), 0)
    j = lax.broadcasted_iota(jnp.int32, (group_size, group_size), 1)

    def as_row(column):
        return jnp.sum(jnp.where(i == j, column, 0), axis=0, keepdims=True)

    def picked(row, mask):
        return jnp.sum(jnp.where(mask, row, 0), axis=1, keepdims=True)

    following = picked(as_row(held), j == lax.rem(i + 1, group_size))
    near = jnp.where((flagged > 0) & (held > 0), following, 0)
    part = picked(as_row(near), j == lax.rem(i + (group_size - 1), group_size))
    shape = 3 * held + near
    shape_row = as_row(shape)
    rank = count((shape_row < shape) | ((shape_row == shape) & (j < i)))
    order = picked(j, as_row(rank) == i)
    starts = count(shape_row < i)
    held_row = as_row(held)
    start_row = as_row(picked(held_row, j < i))
    nth = i - start_row
    mine = (nth >= 0) & (nth < held_row)
    block_source = picked(jnp.where(nth == 0, as_row(low), as_row(high)), mine)
    block_part = count(mine & (as_row(part) > nth))
    place = lax.broadcasted_iota(jnp.int32, table_ref.shape, 1)
    table = jnp.zeros(table_ref.shape, jnp.int32)
    for k, column in enumerate((held, low, high, near, block_part, order, starts, block_source)):
        table = jnp.where(place == k, column, table)
    table_ref[...] = table


def pack_kernel(
    chunk,
    group_size,
    ids_ref,
    row_ref,
    near_ref,
    a_ref,
    b_ref,
    c_ref,
    out_ref,
    table_ref,
    ids,
    row,
    near,
    table,
    held,
    small_sems,
    in_sems,
    out_sems,
):
    per_source = held.shape[0]
    base = lax.axis_index("seq") * per_source
    small = [
        pltpu.make_async_copy(ref, scratch, small_sems.at[k])
        for k, (ref, scratch) in enumerate(((ids_ref, ids), (row_ref, row), (near_ref, near)))
    ]
    for copy in small:
        copy.start()
    arriving, leaving = [], []
    for k in range(per_source // chunk):
        for j, ref in enumerate((a_ref, b_ref, c_ref)):
            blocks = pl.ds(k * chunk, chunk)
            copy = pltpu.make_async_copy(ref.at[blocks], held.at[blocks, j], in_sems.at[k, j])
            copy.start()
            arriving.append(copy)
    for copy in small:
        copy.wait()
    slots = [lax.div(ids[base + i], group_size) for i in range(per_source)]
    for k in range(per_source // chunk):
        for copy in arriving[3 * k : 3 * k + 3]:
            copy.wait()
        for i in range(k * chunk, (k + 1) * chunk):
            copy = pltpu.make_async_copy(held.at[i], out_ref.at[slots[i]], out_sems.at[i])
            copy.start()
            leaving.append(copy)
    make_table(row[...], near[...], group_size, per_source, out_ref.shape[0], table)
    tabled = pltpu.make_async_copy(table, table_ref, small_sems.at[3])
    tabled.start()
    tabled.wait()
    for copy in leaving:
        copy.wait()


def unpack_kernel(chunk, group_size, ids_ref, in_ref, a_ref, b_ref, held, sems):
    per_source = held.shape[1]
    base = lax.axis_index("seq") * per_source
    leaving = []
    for k in range(per_source // chunk):
        for j, ref in enumerate((a_ref, b_ref)):
            for i in range(k * chunk, (k + 1) * chunk):
                held[j, i] = in_ref[lax.div(ids_ref[base + i], group_size), j]
            blocks = pl.ds(k * chunk, chunk)
            copy = pltpu.make_async_copy(held.at[j, blocks], ref.at[blocks], sems.at[k, j])
            copy.start()
            leaving.append(copy)
    for copy in leaving:
        copy.wait()


def attend_kernel(clusters, together, table_ref, in_ref, out_ref, own_ref, part_ref):
    scale = 1.0 / math.sqrt(DH)
    factor = scale * math.log2(math.e)

    def attend(cs, own_count, near_count):
        lanes = range(len(cs))
        own_src = [[table_ref[c, 1 + p] for p in range(own_count)] for c in cs]
        near_src = [
            [table_ref[lax.rem(c + 1, clusters), 1 + p] for p in range(near_count)] for c in cs
        ]

        def load(which, sources):
            return jnp.concatenate([in_ref[s, which] for s in sources], axis=0)

        k = [load(0, own_src[i] + near_src[i]) for i in lanes]
        w = [load(1, own_src[i] + near_src[i]) for i in lanes]
        g = [load(2, own_src[i]) for i in lanes]
        width = own_count * BLOCK
        q = [x[:width] for x in k]
        ahead = lax.broadcasted_iota(jnp.int32, (width, width), 1) - lax.broadcasted_iota(
            jnp.int32, (width, width), 0
        )
        scores = [dot(k[i], q[i], NT) for i in lanes]
        dprobs = [dot(w[i], g[i], NT) for i in lanes]
        own_scores = [jnp.where(ahead == 0, -1e30, x[:width]) for x in scores]
        if near_count:
            scores = [jnp.concatenate([own_scores[i], scores[i][width:]], axis=0) for i in lanes]
        else:
            scores = own_scores
        top = [jnp.max(x, axis=0, keepdims=True) for x in scores]
        weights = [jnp.exp2((scores[i] - top[i]) * factor) for i in lanes]
        inverse = [1.0 / jnp.sum(x, axis=0, keepdims=True) for x in weights]
        delta = [
            jnp.sum(weights[i] * dprobs[i], axis=0, keepdims=True) * inverse[i] for i in lanes
        ]
        probs = [weights[i] * inverse[i] for i in lanes]
        dscores = [(probs[i] * (dprobs[i] - delta[i])).astype(jnp.bfloat16) for i in lanes]
        grad_w = [dot(probs[i].astype(jnp.bfloat16), g[i], NN) for i in lanes]
        grad_k = [dot(dscores[i], q[i], NN) for i in lanes]
        grad_q = [dot(dscores[i], k[i], TN) for i in lanes]
        for i in lanes:
            for p in range(own_count):
                rows = slice(p * BLOCK, (p + 1) * BLOCK)
                own_ref[0, own_src[i][p]] = (grad_q[i][rows] + grad_k[i][rows]) * scale
                own_ref[1, own_src[i][p]] = grad_w[i][rows]
            for p in range(near_count):
                rows = slice(width + p * BLOCK, width + (p + 1) * BLOCK)
                part_ref[0, near_src[i][p]] = grad_k[i][rows] * scale
                part_ref[1, near_src[i][p]] = grad_w[i][rows]

    for own_count in (1, 2):
        for near_count in (0, 1, 2):
            shape = 3 * own_count + near_count
            first, end = table_ref[shape, 6], table_ref[shape + 1, 6]
            lanes = together[shape - 3]

            whole = lax.div(end - first, lanes)
            rest = end - first - whole * lanes

            @pl.loop(0, whole + (rest > 1).astype(jnp.int32))
            def _(turn):
                at = [jnp.minimum(first + turn * lanes + i, end - 1) for i in range(lanes)]
                attend([table_ref[a, 5] for a in at], own_count, near_count)

            @pl.when(rest == 1)
            def _():
                attend([table_ref[end - 1, 5]], own_count, near_count)

    @pl.loop(0, clusters, unroll=True)
    def _(r):
        source = table_ref[r, 7]
        for j in range(2):
            part = jnp.where(table_ref[r, 4] > 0, part_ref[j, source], 0.0)
            out_ref[source, j] = (own_ref[j, source] + part).astype(jnp.bfloat16)


def per_device(shared_qk, values, cotangent, cluster_ids, neighbour):
    n_seq = lax.axis_size("seq")
    tokens, lanes = shared_qk.shape
    per_source = tokens // BLOCK
    group_size = neighbour.shape[0] // n_seq
    dtype = shared_qk.dtype
    any_space = pl.BlockSpec(memory_space=pl.ANY)
    smem = pl.BlockSpec(memory_space=pltpu.SMEM)
    vmem = pl.BlockSpec(memory_space=pltpu.VMEM)

    sent, table = pl.pallas_call(
        functools.partial(pack_kernel, PACK, group_size),
        out_shape=(
            jax.ShapeDtypeStruct((n_seq, 3, BLOCK, lanes), dtype),
            jax.ShapeDtypeStruct((group_size, 128), jnp.int32),
        ),
        in_specs=[any_space] * 6,
        out_specs=(any_space, any_space),
        scratch_shapes=[
            pltpu.SMEM(cluster_ids.shape, jnp.int32),
            pltpu.VMEM((1, cluster_ids.shape[0]), jnp.int32),
            pltpu.VMEM((1, neighbour.shape[0]), jnp.int32),
            pltpu.VMEM((group_size, 128), jnp.int32),
            pltpu.VMEM((per_source, 3, BLOCK, lanes), dtype),
            pltpu.SemaphoreType.DMA((4,)),
            pltpu.SemaphoreType.DMA((per_source // PACK, 3)),
            pltpu.SemaphoreType.DMA((per_source,)),
        ],
        name="pack",
    )(
        cluster_ids,
        cluster_ids.reshape(1, -1),
        neighbour.reshape(1, -1),
        *(x.reshape(-1, BLOCK, lanes) for x in (shared_qk, values, cotangent)),
    )
    arrived = lax.all_to_all(sent, "seq", split_axis=0, concat_axis=0, tiled=True)

    returned = pl.pallas_call(
        functools.partial(attend_kernel, group_size, TOGETHER),
        out_shape=jax.ShapeDtypeStruct((n_seq, 2, BLOCK, lanes), dtype),
        in_specs=[smem, vmem],
        out_specs=vmem,
        scratch_shapes=[
            pltpu.VMEM((2, n_seq, BLOCK, lanes), jnp.float32),
            pltpu.VMEM((2, n_seq, BLOCK, lanes), jnp.float32),
        ],
        compiler_params=pltpu.CompilerParams(vmem_limit_bytes=32 * 1024 * 1024),
        name="attend",
    )(table, arrived)
    home = lax.all_to_all(returned, "seq", split_axis=0, concat_axis=0, tiled=True)

    out = jax.ShapeDtypeStruct((per_source, BLOCK, lanes), dtype)
    grads = pl.pallas_call(
        functools.partial(unpack_kernel, UNPACK, group_size),
        out_shape=(out, out),
        in_specs=[smem, vmem],
        out_specs=(any_space, any_space),
        scratch_shapes=[
            pltpu.VMEM((2, per_source, BLOCK, lanes), dtype),
            pltpu.SemaphoreType.DMA((per_source // UNPACK, 2)),
        ],
        compiler_params=pltpu.CompilerParams(vmem_limit_bytes=8 * 1024 * 1024),
        name="unpack",
    )(cluster_ids, home)
    return tuple(x.reshape(tokens, lanes) for x in grads)


def solution(mesh):
    in_specs = (P("seq", "head"), P("seq", "head"), P("seq", "head"), P(), P())
    out_specs = (P("seq", "head"), P("seq", "head"))
    return jax.shard_map(
        per_device, mesh=mesh, in_specs=in_specs, out_specs=out_specs, check_vma=False
    )
```
